128 devices in a mesh: sp: 32 (over z, y, core), kv: 4 (over x).
Axes of the slice: x: 4, y: 4, z: 4, core: 2. Of those that a mesh axis runs over, the one named last changes fastest.
Arguments:
- query_states: bfloat16 [8192, 3584], P('sp', 'kv'), may hold values from -17 to 17
- key_states: bfloat16 [8192, 512], P('sp', 'kv'), may hold values from -17 to 17
- loader_value_rows: bfloat16 [8192, 512], P('sp', 'kv'), may hold values from -6 to 6
- group_sizes: int32 [16], replicated, may hold values from 1 to 8, 32 in all
- out_weight: bfloat16 [3584, 3584], P(None, 'kv'), may hold values from -0.09375 to 0.09375
Outputs:
- layer_output: bfloat16 [8192, 3584], P('sp', 'kv')
The draws below stay inside these ranges and needn't reach their ends.
Inputs may be any that keep to these rules, and one draw needn't show every extreme that they name: `group_sizes`: the entries sum to 32, and the largest is exactly 8.
All inputs are finite; a program needn't handle non-finite values.
Results may differ from the reference program's by a relative error of at most 0.0055.
Values may be sent and summed in bfloat16 or wider, within the bound.
A program may use at most 192 MiB of HBM per device.

```python
import math
import jax
import jax.numpy as jnp
import numpy as np
from jax import lax

D = 3584
QUERY_HEADS = 28
KEY_VALUE_HEADS = 4
HEAD_FEATURES = 128
TOK_DEV = 256
GMAX = 8
SEQS = 16
BLOCK = 8
TOKEN_ROWS_TOTAL = 8192
N_SP = 32


def into_loader_layout(packed):
    columns = packed.shape[1]
    return packed.reshape(N_SP, N_SP, BLOCK, columns).transpose(1, 0, 2, 3).reshape(TOKEN_ROWS_TOTAL, columns)


def draw_query_states(key, part):
    key = jax.random.fold_in(key, 23)
    group_head_count = QUERY_HEADS // KEY_VALUE_HEADS
    drawn_reference = 1.7 * jnp.clip(jax.random.normal(key, (TOKEN_ROWS_TOTAL, KEY_VALUE_HEADS, group_head_count, HEAD_FEATURES), jnp.float32), -4.0, 4.0)
    return into_loader_layout(drawn_reference.reshape(TOKEN_ROWS_TOTAL, QUERY_HEADS * HEAD_FEATURES)).astype(jnp.bfloat16)


def draw_key_states(key, part):
    key = jax.random.fold_in(key, 11)
    drawn_reference = 1.7 * jnp.clip(jax.random.normal(key, (TOKEN_ROWS_TOTAL, KEY_VALUE_HEADS, HEAD_FEATURES), jnp.float32), -4.0, 4.0)
    return into_loader_layout(drawn_reference.reshape(TOKEN_ROWS_TOTAL, KEY_VALUE_HEADS * HEAD_FEATURES)).astype(jnp.bfloat16)


def block_scale(stream_key, extent, pieces, smallest, largest):
    def one(axis_at, parts):
        heights = jax.random.uniform(jax.random.fold_in(jax.random.fold_in(stream_key, 6), axis_at), (parts,), jnp.float32, smallest / len(pieces), largest / len(pieces))
        return jnp.repeat(jnp.exp(heights), extent[axis_at] // parts).reshape((-1,) + (1,) * (len(extent) - axis_at - 1))

    level = one(*pieces[0])
    for cut in pieces[1:]:
        level = level * one(*cut)
    return level


def split_up(count, total, limit, skew):
    loads = [(1 << 20) // math.isqrt(grade ** skew) + 1 for grade in range(2, count + 1)]
    rest, holding = total - limit - (count - 1), [1] * (count - 1)
    while rest > 0:
        movable = [i for i in range(count - 1) if holding[i] < limit]
        whole, remaining = sum([loads[i] for i in movable]), rest
        for i in movable:
            more = min(limit - holding[i], max(1, remaining * loads[i] // whole), rest)
            holding[i] = holding[i] + more
            rest = rest - more
    return np.array([limit] + holding)


def ragged(own_key, count, total, reach, lean):
    if count == 2:
        one = jax.random.randint(own_key, (), max(1, total - reach), min(reach, total - 1) + 1)
        return jnp.stack([one, total - one])
    tallies = jnp.asarray(split_up(count, total, reach, lean), jnp.int32)
    twos = (count - 1) // 2
    source_of, receiver = tallies[1:1 + 2 * twos:2], tallies[2:2 + 2 * twos:2]
    room = jnp.minimum(source_of - 1, reach - receiver)
    shifted = jax.random.randint(jax.random.fold_in(own_key, 1), (twos,), 0, 1 << 20) % (room + 1)
    tallies = tallies.at[1:1 + 2 * twos:2].set(source_of - shifted).at[2:2 + 2 * twos:2].set(receiver + shifted)
    return tallies[jax.random.permutation(jax.random.fold_in(own_key, 2), count)]


def noise(rng, dims, scale, reach, cuts=(), kind=jnp.bfloat16):
    factor_of = block_scale(rng, dims, cuts, -0.22, 0.18) if cuts else 1.0
    values = jax.random.normal(rng, dims, jnp.float32) * scale * factor_of
    return jnp.minimum(jnp.maximum(values, -reach), reach).astype(kind)


def setup_inputs(seed: int = 0) -> dict:
    seeds = jax.random.split(jax.random.key(seed), 6)
    query_states = draw_query_states(jax.random.fold_in(seeds[5], 71), 0)
    key_states = draw_key_states(jax.random.fold_in(seeds[5], 71), 0)
    loader_value_rows = noise(seeds[2], (TOKEN_ROWS_TOTAL, KEY_VALUE_HEADS * HEAD_FEATURES), 1.0, 6.0, ((0, 32), (1, 4)))
    group_sizes = ragged(seeds[3], SEQS, N_SP, GMAX, 2).astype(jnp.int32)
    out_weight = noise(seeds[4], (QUERY_HEADS * HEAD_FEATURES, D), (QUERY_HEADS * HEAD_FEATURES) ** -0.5, 0.09375, ((1, 4),))
    return {"query_states": query_states, "key_states": key_states, "loader_value_rows": loader_value_rows, "group_sizes": group_sizes, "out_weight": out_weight}


def loader_swap(array):
    columns = array.shape[1]
    return array.reshape(N_SP, N_SP, BLOCK, columns).transpose(1, 0, 2, 3).reshape(TOKEN_ROWS_TOTAL, columns)


def reference(query_states, key_states, loader_value_rows, group_sizes, out_weight):
    packed_q = loader_swap(query_states)
    packed_k = loader_swap(key_states)
    packed_v = loader_swap(loader_value_rows)
    group_ends = jnp.cumsum(group_sizes).astype(jnp.int32)
    group_begins = (group_ends - group_sizes).astype(jnp.int32)
    round_ids = jnp.arange(N_SP, dtype=jnp.int32)
    inside = (group_begins[None, :] <= round_ids[:, None]) & (round_ids[:, None] < group_ends[None, :])
    first_device = jnp.sum(jnp.where(inside, group_begins[None, :], 0), axis=1).astype(jnp.int32)
    window_rows = GMAX * TOK_DEV
    group_head_count = QUERY_HEADS // KEY_VALUE_HEADS

    def one_round(round_id):
        query_rows = lax.dynamic_slice_in_dim(packed_q, round_id * TOK_DEV, TOK_DEV, 0)
        key_begin = jnp.clip((round_id + 1 - GMAX) * TOK_DEV, 0, TOKEN_ROWS_TOTAL - window_rows).astype(jnp.int32)
        key_rows = lax.dynamic_slice_in_dim(packed_k, key_begin, window_rows, 0)
        value_rows = lax.dynamic_slice_in_dim(packed_v, key_begin, window_rows, 0)
        query_ids = round_id * TOK_DEV + jnp.arange(TOK_DEV, dtype=jnp.int32)
        key_ids = key_begin + jnp.arange(window_rows, dtype=jnp.int32)
        seq_first = first_device[round_id] * TOK_DEV
        visible = (key_ids[None, :] <= query_ids[:, None]) & (key_ids[None, :] >= seq_first)

        def single_head_group(group_id):
            group_queries = lax.dynamic_slice_in_dim(query_rows, group_id * group_head_count * HEAD_FEATURES, group_head_count * HEAD_FEATURES, 1)
            group_queries = group_queries.reshape(TOK_DEV, group_head_count, HEAD_FEATURES).astype(jnp.float32)
            group_keys = lax.dynamic_slice_in_dim(key_rows, group_id * HEAD_FEATURES, HEAD_FEATURES, 1).astype(jnp.float32)
            group_values = lax.dynamic_slice_in_dim(value_rows, group_id * HEAD_FEATURES, HEAD_FEATURES, 1).astype(jnp.float32)
            scores = jnp.einsum("qhd,kd->qhk", group_queries, group_keys) * (HEAD_FEATURES ** -0.5)
            scores = jnp.where(visible[:, None, :], scores, -jnp.inf)
            row_top = jnp.max(scores, axis=2, keepdims=True)
            exact = jnp.exp(scores - row_top)
            row_total = jnp.sum(exact, axis=2)
            rounded = lax.optimization_barrier(exact.astype(jnp.bfloat16))
            weighted = jnp.einsum("qhk,kd->qhd", rounded.astype(jnp.float32), group_values)
            return (weighted / row_total[:, :, None]).reshape(TOK_DEV, group_head_count * HEAD_FEATURES)

        within_group = lax.map(single_head_group, jnp.arange(KEY_VALUE_HEADS, dtype=jnp.int32))
        return within_group.transpose(1, 0, 2).reshape(TOK_DEV, QUERY_HEADS * HEAD_FEATURES).astype(jnp.bfloat16)

    attended = lax.map(one_round, round_ids).reshape(TOKEN_ROWS_TOTAL, QUERY_HEADS * HEAD_FEATURES)
    attended_loader = loader_swap(attended)
    return jnp.dot(attended_loader, out_weight, preferred_element_type=jnp.float32).astype(jnp.bfloat16)
```

```python
import functools

import jax
import jax.numpy as jnp
from jax import lax
from jax.experimental import pallas as pl
from jax.experimental.pallas import tpu as pltpu
from jax.sharding import PartitionSpec as P

MESH = pl.DeviceIdType.MESH
ROWS, FEAT, COLS, HEADS = 256, 128, 896, 7
PAIR = 16
KEYS = 512
LOG2E = 1.4426950408889634
CHUNKS = ((0, 64), (64, 64), (128, 64), (192, 64))
N_SEM = 128


def nxt(a, by):
    return lax.rem(a + by, 4)


def attention_kernel(
    q_ref, k_ref, v_ref, gs_ref, w_ref, o_ref,
    qv, kb, vb, xa, wv, acc, first, ssem, rsem, lsem,
):
    sp = lax.axis_index("sp")
    x = lax.axis_index("kv")
    c = lax.rem(sp, 2)
    y = lax.rem(sp // 2, 4)
    z = sp // 8

    def dev(z_, y_, c_, x_):
        return ((z_ * 4 + y_) * 2 + c_, x_)

    along_y = [dev(z, nxt(y, d), c, x) for d in (1, 3, 2)]
    along_z = [dev(nxt(z, d), y, c, x) for d in (1, 3, 2)]
    along_x = [dev(z, y, c, nxt(x, d)) for d in (1, 3, 2)]
    sibling = dev(z, y, 1 - c, x)

    peers = along_y + along_z + along_x + [sibling]
    barrier = pltpu.get_barrier_semaphore()
    for d in peers:
        pl.semaphore_signal(barrier, inc=1, device_id=d, device_id_type=MESH)
    pl.semaphore_wait(barrier, len(peers))

    ids = {}
    pending = []

    def remote(key, src, dst, d):
        i = ids.setdefault(key, len(ids))
        return pltpu.make_async_remote_copy(
            src_ref=src, dst_ref=dst, send_sem=ssem.at[i], recv_sem=rsem.at[i],
            device_id=d, device_id_type=MESH,
        )

    def send(key, src, dst, d):
        r = remote(key, src, dst, d)
        r.start()
        pending.append(r)

    def recv(key, dst):
        remote(key, dst, dst, sibling).wait_recv()

    src = {"k": k_ref, "v": v_ref}

    def shard(t, f, r0, n):
        if t == "k":
            return kb.at[z, f, c, pl.ds(r0, n)]
        return vb.at[f, y, c, pl.ds(r0, n)]

    def line(t, s, core, r0, n):
        if t == "k":
            return kb.at[s, :, core, pl.ds(r0, n)]
        return vb.at[:, s, core, pl.ds(r0, n)]

    def firsts(t):
        return (y, along_y) if t == "k" else (z, along_z)

    def seconds(t):
        return (z, along_z) if t == "k" else (y, along_y)

    def own_copy(t, ci):
        r0, n = CHUNKS[ci]
        f, _ = firsts(t)
        return pltpu.make_async_copy(
            src[t].at[pl.ds(r0, n)], shard(t, f, r0, n), lsem.at[2 * ci + (t == "v")]
        )

    def kv_first(ci):
        r0, n = CHUNKS[ci]
        for t in "kv":
            f, to = firsts(t)
            for i in range(3):
                send((t, ci, "f", i), src[t].at[pl.ds(r0, n)], shard(t, f, r0, n), to[i])
            own_copy(t, ci).start()

    def kv_second(ci):
        r0, n = CHUNKS[ci]
        for t in "kv":
            f, _ = firsts(t)
            s, to = seconds(t)
            for i, d in enumerate((3, 1, 2)):
                recv((t, ci, "f", i), shard(t, nxt(f, d), r0, n))
            own_copy(t, ci).wait()
            mine = line(t, s, c, r0, n)
            for i in range(3):
                send((t, ci, "s", i), mine, mine, to[i])
            send((t, ci, "c", 3), mine, mine, sibling)

    def kv_share(ci):
        r0, n = CHUNKS[ci]
        for i, d in enumerate((3, 1, 2)):
            for t in "kv":
                s, _ = seconds(t)
                got = line(t, nxt(s, d), c, r0, n)
                recv((t, ci, "s", i), got)
                send((t, ci, "c", i), got, got, sibling)

    def kv_ready(ci):
        r0, n = CHUNKS[ci]
        for i, d in enumerate((3, 1, 2, 0)):
            for t in "kv":
                s, _ = seconds(t)
                recv((t, ci, "c", i), line(t, nxt(s, d), 1 - c, r0, n))

    def halves(ci):
        r0, n = CHUNKS[ci]
        return pl.ds(r0, n // 2), pl.ds(r0 + n // 2, n // 2)

    def x_send(ci):
        a, b = halves(ci)
        right, left, _ = along_x
        send(("x", ci, "ra"), xa.at[0, a], xa.at[1, a], right)
        send(("x", ci, "lb"), xa.at[0, b], xa.at[2, b], left)
        send(("x", ci, "rb"), xa.at[0, b], xa.at[1, b], right)
        send(("x", ci, "la"), xa.at[0, a], xa.at[2, a], left)

    def x_forward(ci):
        a, b = halves(ci)
        right, left, _ = along_x
        recv(("x", ci, "ra"), xa.at[1, a])
        send(("x", ci, "fa"), xa.at[1, a], xa.at[3, a], right)
        recv(("x", ci, "lb"), xa.at[2, b])
        send(("x", ci, "fb"), xa.at[2, b], xa.at[3, b], left)

    def x_near(ci):
        a, b = halves(ci)
        recv(("x", ci, "rb"), xa.at[1, b])
        recv(("x", ci, "la"), xa.at[2, a])

    def x_far(ci):
        a, b = halves(ci)
        recv(("x", ci, "fa"), xa.at[3, a])
        recv(("x", ci, "fb"), xa.at[3, b])

    kv_first(0)
    q_copy = pltpu.make_async_copy(q_ref, qv, lsem.at[8])
    q_copy.start()
    for ci in range(1, len(CHUNKS)):
        kv_first(ci)
    w_copies = [
        pltpu.make_async_copy(
            w_ref.at[pl.ds(nxt(x, d) * COLS, COLS)], wv.at[i], lsem.at[9 + i]
        )
        for i, d in enumerate((0, 3, 1, 2))
    ]
    for w in w_copies:
        w.start()

    sizes = [gs_ref[i] for i in range(16)]

    @pl.loop(0, 32)
    def _(b):
        begin, total = 0, 0
        for size in sizes:
            begin = jnp.where(total <= b, total, begin)
            total = total + size
        first[b] = begin

    q_copy.wait()

    def attend(p, window):
        width = window * KEYS
        rows = pl.ds(pl.multiple_of(p * PAIR, PAIR), PAIR)
        q = jnp.concatenate([qv[rows, h * FEAT : (h + 1) * FEAT] for h in range(HEADS)], axis=0)
        lane = lax.broadcasted_iota(jnp.int32, (8, width), 1)
        sub = lax.broadcasted_iota(jnp.int32, (8, width), 0)
        key_id = (
            (lane // KEYS - (window - 1)) * KEYS
            + ((lane // 8) % 2) * 256 + ((lane % KEYS) // 16) * 8 + lane % 8
        )
        biases = []
        for half in range(2):
            low = first[2 * p + half] * 256 - p * KEYS
            high = half * 256 + sp * 8 + sub
            biases.append(jnp.where((key_id >= low) & (key_id <= high), 0.0, -1e30))
        bias = jnp.stack(biases)
        parts = []
        for j in range(window):
            at = pl.ds(pl.multiple_of((p - (window - 1) + j) * PAIR, PAIR), PAIR)
            keys = kb[:, :, :, at, :].reshape(KEYS, FEAT)
            parts.append(
                lax.dot_general(q, keys, (((1,), (1,)), ((), ())), preferred_element_type=jnp.float32)
            )
        scores = jnp.concatenate(parts, axis=1) if window > 1 else parts[0]
        scores = scores * (LOG2E * FEAT**-0.5)
        scores = (scores.reshape(HEADS, 2, 8, width) + bias[None]).reshape(HEADS * PAIR, width)
        top = jnp.max(scores, axis=1, keepdims=True)
        powers = jnp.exp2(scores - top)
        total = jnp.sum(powers, axis=1, keepdims=True)
        powers = powers.astype(jnp.bfloat16)
        out = jnp.zeros((HEADS * PAIR, FEAT), jnp.float32)
        for j in range(window):
            at = pl.ds(pl.multiple_of((p - (window - 1) + j) * PAIR, PAIR), PAIR)
            values = vb[:, :, :, at, :].reshape(KEYS, FEAT)
            out = out + jnp.dot(
                powers[:, j * KEYS : (j + 1) * KEYS], values, preferred_element_type=jnp.float32
            )
        out = (out / total).astype(jnp.bfloat16)
        for h in range(HEADS):
            xa[0, rows, h * FEAT : (h + 1) * FEAT] = out[h * PAIR : (h + 1) * PAIR]

    def attend_chunk(ci):
        r0, n = CHUNKS[ci]
        if ci == 0:
            for p in range(n // PAIR):
                attend(p, p + 1)
        else:
            @pl.loop(r0 // PAIR, (r0 + n) // PAIR)
            def _(p):
                attend(p, 5)

    def project(slot, r0, n, start=False):
        part = jnp.dot(xa[slot, r0 : r0 + n], wv[slot], preferred_element_type=jnp.float32)
        if start:
            acc[r0 : r0 + n] = part
        else:
            acc[r0 : r0 + n] += part

    kv_second(0)
    kv_second(1)
    kv_share(0)
    kv_second(2)
    kv_ready(0)
    attend_chunk(0)
    x_send(0)
    kv_second(3)
    kv_share(1)
    kv_ready(1)
    attend_chunk(1)
    x_send(1)
    kv_share(2)
    x_forward(0)
    kv_ready(2)
    attend_chunk(2)
    x_send(2)
    kv_share(3)
    x_forward(1)
    kv_ready(3)
    attend_chunk(3)
    x_send(3)
    for w in w_copies:
        w.wait()
    project(0, 0, 128, start=True)
    x_forward(2)
    project(0, 128, 128, start=True)
    x_near(0)
    x_near(1)
    project(1, 0, 128)
    x_forward(3)
    project(2, 0, 128)
    x_far(0)
    x_far(1)
    project(3, 0, 128)
    x_near(2)
    x_near(3)
    project(1, 128, 128)
    project(2, 128, 128)
    x_far(2)
    x_far(3)
    project(3, 128, 128)
    o_ref[...] = acc[...].astype(jnp.bfloat16)
    for r in pending:
        r.wait_send()


def on_device(query_states, key_states, loader_value_rows, group_sizes, out_weight):
    anywhere = pl.BlockSpec(memory_space=pl.ANY)
    gathered = pltpu.VMEM((4, 4, 2, ROWS, FEAT), jnp.bfloat16)
    return pl.pallas_call(
        attention_kernel,
        out_shape=jax.ShapeDtypeStruct((ROWS, COLS), jnp.bfloat16),
        in_specs=[anywhere, anywhere, anywhere, pl.BlockSpec(memory_space=pltpu.SMEM), anywhere],
        out_specs=pl.BlockSpec(memory_space=pltpu.VMEM),
        scratch_shapes=[
            pltpu.VMEM((ROWS, COLS), jnp.bfloat16),
            gathered,
            gathered,
            pltpu.VMEM((4, ROWS, COLS), jnp.bfloat16),
            pltpu.VMEM((4, COLS, COLS), jnp.bfloat16),
            pltpu.VMEM((ROWS, COLS), jnp.float32),
            pltpu.SMEM((32,), jnp.int32),
            pltpu.SemaphoreType.DMA((N_SEM,)),
            pltpu.SemaphoreType.DMA((N_SEM,)),
            pltpu.SemaphoreType.DMA((16,)),
        ],
        compiler_params=pltpu.CompilerParams(
            collective_id=0, has_side_effects=True, vmem_limit_bytes=56 << 20
        ),
    )(query_states, key_states, loader_value_rows, group_sizes, out_weight)


def solution(mesh):
    return jax.shard_map(
        on_device,
        mesh=mesh,
        in_specs=(P("sp", "kv"), P("sp", "kv"), P("sp", "kv"), P(), P(None, "kv")),
        out_specs=P("sp", "kv"),
        check_vma=False,
    )
```

```python
import functools

import jax
import jax.numpy as jnp
from jax import lax
from jax.experimental import pallas as pl
from jax.experimental.pallas import tpu as pltpu
from jax.sharding import PartitionSpec as P

MESH = pl.DeviceIdType.MESH
ROWS, FEAT, COLS, HEADS = 256, 128, 896, 7
PAIR = 16
KEYS = 512
LOG2E = 1.4426950408889634
QUAD = 32
CHUNKS = ((0, 64), (64, 64), (128, 64), (192, 64))
N_SEM = 26 * len(CHUNKS)
SCALE = LOG2E * FEAT**-0.5
NT = (((1,), (1,)), ((), ()))


def nxt(a, by):
    return lax.rem(a + by, 4)


def by_lanes(op, a):
    return op(op(a[:, :128], a[:, 128:256]), op(a[:, 256:384], a[:, 384:]))


def attention_kernel(
    q_ref, k_ref, v_ref, gs_ref, w_ref, o_ref,
    qv, kb, vb, xa, wv, acc, ov, sizes, first, ssem, rsem, lsem,
):
    sp = lax.axis_index("sp")
    x = lax.axis_index("kv")
    c = lax.rem(sp, 2)
    y = lax.rem(sp // 2, 4)
    z = sp // 8

    def dev(z_, y_, c_, x_):
        return ((z_ * 4 + y_) * 2 + c_, x_)

    along_y = [dev(z, nxt(y, d), c, x) for d in (1, 3, 2)]
    along_z = [dev(nxt(z, d), y, c, x) for d in (1, 3, 2)]
    along_x = [dev(z, y, c, nxt(x, d)) for d in (1, 3, 2)]
    sibling = dev(z, y, 1 - c, x)

    peers = along_y + along_z + along_x + [sibling]
    barrier = pltpu.get_barrier_semaphore()
    for d in peers:
        pl.semaphore_signal(barrier, inc=1, device_id=d, device_id_type=MESH)
    size_copy = pltpu.make_async_copy(gs_ref, sizes, lsem.at[0])
    size_copy.start()
    q_copy = pltpu.make_async_copy(q_ref, qv, lsem.at[1])
    q_copy.start()
    w_copies = [
        pltpu.make_async_copy(
            w_ref.at[pl.ds(nxt(x, d) * COLS, COLS)], wv.at[i], lsem.at[2 + i]
        )
        for i, d in enumerate((0, 3, 1, 2))
    ]
    for w in w_copies:
        w.start()
    pl.semaphore_wait(barrier, len(peers))

    ids = {}
    pending = []

    def remote(key, src, dst, d):
        i = ids.setdefault(key, len(ids))
        return pltpu.make_async_remote_copy(
            src_ref=src, dst_ref=dst, send_sem=ssem.at[i], recv_sem=rsem.at[i],
            device_id=d, device_id_type=MESH,
        )

    def send(key, src, dst, d):
        r = remote(key, src, dst, d)
        r.start()
        pending.append(r)

    def recv(key, dst):
        remote(key, dst, dst, sibling).wait_recv()

    src = {"k": k_ref, "v": v_ref}

    def shard(t, f, r0, n):
        if t == "k":
            return kb.at[z, f, c, pl.ds(r0, n)]
        return vb.at[f, y, c, pl.ds(r0, n)]

    def line(t, s, core, r0, n):
        if t == "k":
            return kb.at[s, :, core, pl.ds(r0, n)]
        return vb.at[:, s, core, pl.ds(r0, n)]

    def firsts(t):
        return (y, along_y) if t == "k" else (z, along_z)

    def seconds(t):
        return (z, along_z) if t == "k" else (y, along_y)

    def own_copy(t, ci):
        r0, n = CHUNKS[ci]
        f, _ = firsts(t)
        return pltpu.make_async_copy(
            src[t].at[pl.ds(r0, n)], shard(t, f, r0, n), lsem.at[8 + 2 * ci + (t == "v")]
        )

    def kv_first(ci):
        r0, n = CHUNKS[ci]
        for t in "kv":
            f, to = firsts(t)
            for i in range(3):
                send((t, ci, "f", i), src[t].at[pl.ds(r0, n)], shard(t, f, r0, n), to[i])
            own_copy(t, ci).start()

    def kv_second(ci):
        r0, n = CHUNKS[ci]
        for t in "kv":
            f, _ = firsts(t)
            s, to = seconds(t)
            for i, d in enumerate((3, 1, 2)):
                recv((t, ci, "f", i), shard(t, nxt(f, d), r0, n))
            own_copy(t, ci).wait()
            mine = line(t, s, c, r0, n)
            for i in range(3):
                send((t, ci, "s", i), mine, mine, to[i])
            send((t, ci, "c", 3), mine, mine, sibling)

    def kv_share(ci):
        r0, n = CHUNKS[ci]
        for i, d in enumerate((3, 1, 2)):
            for t in "kv":
                s, _ = seconds(t)
                got = line(t, nxt(s, d), c, r0, n)
                recv((t, ci, "s", i), got)
                send((t, ci, "c", i), got, got, sibling)

    def kv_ready(ci):
        r0, n = CHUNKS[ci]
        for i, d in enumerate((3, 1, 2, 0)):
            for t in "kv":
                s, _ = seconds(t)
                recv((t, ci, "c", i), line(t, nxt(s, d), 1 - c, r0, n))

    def halves(ci):
        r0, n = CHUNKS[ci]
        return pl.ds(r0, n // 2), pl.ds(r0 + n // 2, n // 2)

    def x_send(ci):
        a, b = halves(ci)
        right, left, _ = along_x
        send(("x", ci, "ra"), xa.at[0, a], xa.at[1, a], right)
        send(("x", ci, "lb"), xa.at[0, b], xa.at[2, b], left)
        send(("x", ci, "rb"), xa.at[0, b], xa.at[1, b], right)
        send(("x", ci, "la"), xa.at[0, a], xa.at[2, a], left)

    def x_forward(ci):
        a, b = halves(ci)
        right, left, _ = along_x
        recv(("x", ci, "ra"), xa.at[1, a])
        send(("x", ci, "fa"), xa.at[1, a], xa.at[3, a], right)
        recv(("x", ci, "lb"), xa.at[2, b])
        send(("x", ci, "fb"), xa.at[2, b], xa.at[3, b], left)

    def x_near(ci):
        a, b = halves(ci)
        recv(("x", ci, "rb"), xa.at[1, b])
        recv(("x", ci, "la"), xa.at[2, a])

    def x_far(ci):
        a, b = halves(ci)
        recv(("x", ci, "fa"), xa.at[3, a])
        recv(("x", ci, "fb"), xa.at[3, b])

    def make_table():
        size_copy.wait()
        listed = [sizes[i] for i in range(16)]

        @pl.loop(0, 32)
        def _(b):
            begin, total = 0, 0
            for size in listed:
                begin = jnp.where(total <= b, total, begin)
                total = total + size
            first[b] = begin

    def pair_rows(p):
        return pl.ds(p * PAIR, PAIR)

    def gathered(ref, p):
        return ref[:, :, :, pair_rows(p), :].reshape(KEYS, FEAT)

    def pair_bias(p, kp):
        lane = lax.broadcasted_iota(jnp.int32, (8, KEYS), 1)
        sub = lax.broadcasted_iota(jnp.int32, (8, KEYS), 0)
        key_id = kp * KEYS + ((lane // 8) % 2) * 256 + (lane // 16) * 8 + lane % 8
        biases = []
        for half in range(2):
            seen = key_id >= first[2 * p + half] * 256
            if kp == p:
                seen = seen & (key_id <= p * KEYS + half * 256 + sp * 8 + sub)
            biases.append(jnp.where(seen, 0.0, -1e30))
        return jnp.stack(biases)

    def scored(q, p_list, kp):
        s = lax.dot_general(q, gathered(kb, kp), NT, preferred_element_type=jnp.float32)
        bias = jnp.stack([pair_bias(p, kp)[None] for p in p_list])
        return (s.reshape(len(p_list), HEADS, 2, 8, KEYS) + bias).reshape(s.shape)

    def attend(t):
        m = HEADS * PAIR
        p0, p1 = 2 * t, 2 * t + 1
        q = jnp.concatenate(
            [qv[pair_rows(p), h * FEAT : (h + 1) * FEAT] for p in (p0, p1) for h in range(HEADS)], axis=0
        )
        middle = range(max(0, p0 - 3), p0 + 1)
        both = [scored(q, (p0, p1), kp) for kp in middle]
        edge1 = scored(q[m:], (p1,), p1)
        top1 = by_lanes(jnp.maximum, edge1)
        edge0 = None
        if p0 >= 4:
            edge0 = scored(q[:m], (p0,), p0 - 4)
            tops = jnp.concatenate([by_lanes(jnp.maximum, edge0), top1], axis=0)
        else:
            tops = jnp.concatenate([jnp.full((m, 128), -1e30, jnp.float32), top1], axis=0)
        for s in both:
            tops = jnp.maximum(tops, by_lanes(jnp.maximum, s))
        top = jnp.max(tops, axis=1, keepdims=True) * SCALE
        powers = jnp.exp2(edge1 * SCALE - top[m:])
        total1 = by_lanes(jnp.add, powers)
        out1 = jnp.dot(powers.astype(jnp.bfloat16), gathered(vb, p1), preferred_element_type=jnp.float32)
        if edge0 is not None:
            powers = jnp.exp2(edge0 * SCALE - top[:m])
            total0 = by_lanes(jnp.add, powers)
            out0 = jnp.dot(
                powers.astype(jnp.bfloat16), gathered(vb, p0 - 4), preferred_element_type=jnp.float32
            )
        else:
            total0 = jnp.zeros((m, 128), jnp.float32)
            out0 = jnp.zeros((m, FEAT), jnp.float32)
        total = jnp.concatenate([total0, total1], axis=0)
        out = jnp.concatenate([out0, out1], axis=0)
        for s, kp in zip(both, middle):
            powers = jnp.exp2(s * SCALE - top)
            total = total + by_lanes(jnp.add, powers)
            out = out + jnp.dot(
                powers.astype(jnp.bfloat16), gathered(vb, kp), preferred_element_type=jnp.float32
            )
        out = (out / jnp.sum(total, axis=1, keepdims=True)).astype(jnp.bfloat16)
        for i, p in enumerate((p0, p1)):
            for h in range(HEADS):
                at = i * m + h * PAIR
                xa[0, pair_rows(p), h * FEAT : (h + 1) * FEAT] = out[at : at + PAIR]

    def attend_chunk(ci):
        r0, n = CHUNKS[ci]
        for t in range(r0 // QUAD, (r0 + n) // QUAD):
            attend(t)

    def project(slot, r0, n, start=False):
        part = jnp.dot(xa[slot, r0 : r0 + n], wv[slot], preferred_element_type=jnp.float32)
        if start:
            acc[r0 : r0 + n] = part
        else:
            acc[r0 : r0 + n] += part

    out_copies = []

    def put_out(r0, n):
        ov[r0 : r0 + n] = acc[r0 : r0 + n].astype(jnp.bfloat16)
        copy = pltpu.make_async_copy(
            ov.at[pl.ds(r0, n)], o_ref.at[pl.ds(r0, n)], lsem.at[8 + 2 * len(CHUNKS) + len(out_copies)]
        )
        copy.start()
        out_copies.append(copy)

    count = len(CHUNKS)

    def step(what, ci):
        if 0 <= ci < count:
            what(ci)

    for i in range(count):
        kv_first(i)
    make_table()
    q_copy.wait()
    for i in range(count):
        kv_second(i)
    for i in range(count):
        kv_share(i)
        step(x_forward, i - 2)
        kv_ready(i)
        attend_chunk(i)
        x_send(i)
    for w in w_copies:
        w.wait()
    project(0, 0, 256, start=True)
    x_forward(count - 2)
    half = 2
    for i in range(half):
        x_near(i)
    project(1, 0, 128)
    x_forward(count - 1)
    project(2, 0, 128)
    for i in range(half):
        x_far(i)
    project(3, 0, 128)
    put_out(0, 128)
    for i in range(half, count):
        x_near(i)
    project(1, 128, 128)
    project(2, 128, 128)
    for i in range(half, count):
        x_far(i)
    project(3, 128, 128)
    put_out(128, 128)
    for copy in out_copies:
        copy.wait()
    for r in pending:
        r.wait_send()


def on_device(query_states, key_states, loader_value_rows, group_sizes, out_weight):
    anywhere = pl.BlockSpec(memory_space=pl.ANY)
    gathered = pltpu.VMEM((4, 4, 2, ROWS, FEAT), jnp.bfloat16)
    return pl.pallas_call(
        attention_kernel,
        out_shape=jax.ShapeDtypeStruct((ROWS, COLS), jnp.bfloat16),
        in_specs=[anywhere] * 5,
        out_specs=anywhere,
        scratch_shapes=[
            pltpu.VMEM((ROWS, COLS), jnp.bfloat16),
            gathered,
            gathered,
            pltpu.VMEM((4, ROWS, COLS), jnp.bfloat16),
            pltpu.VMEM((4, COLS, COLS), jnp.bfloat16),
            pltpu.VMEM((ROWS, COLS), jnp.float32),
            pltpu.VMEM((ROWS, COLS), jnp.bfloat16),
            pltpu.SMEM((16,), jnp.int32),
            pltpu.SMEM((32,), jnp.int32),
            pltpu.SemaphoreType.DMA((N_SEM,)),
            pltpu.SemaphoreType.DMA((N_SEM,)),
            pltpu.SemaphoreType.DMA((16 + 2 * len(CHUNKS),)),
        ],
        compiler_params=pltpu.CompilerParams(
            collective_id=0, has_side_effects=True, vmem_limit_bytes=56 << 20
        ),
    )(query_states, key_states, loader_value_rows, group_sizes, out_weight)


def solution(mesh):
    return jax.shard_map(
        on_device,
        mesh=mesh,
        in_specs=(P("sp", "kv"), P("sp", "kv"), P("sp", "kv"), P(), P(None, "kv")),
        out_specs=P("sp", "kv"),
        check_vma=False,
    )
```

```python
import functools

import jax
import jax.numpy as jnp
from jax import lax
from jax.experimental import pallas as pl
from jax.experimental.pallas import tpu as pltpu
from jax.sharding import PartitionSpec as P

MESH = pl.DeviceIdType.MESH
ROWS, FEAT, COLS, HEADS = 256, 128, 896, 7
PAIR = 16
KEYS = 512
LOG2E = 1.4426950408889634
QUAD = 32
CHUNK_ROWS = (64, 64, 64, 64)
CHUNKS = tuple((sum(CHUNK_ROWS[:i]), n) for i, n in enumerate(CHUNK_ROWS))
KV_RELAY = (0, 0, 1, 1)
X_RELAY = (1, 1, 1, 1)
TAIL = 1
UNIT_ROWS = (64, 64, 64, 64)
UNITS = tuple((sum(UNIT_ROWS[:i]), n) for i, n in enumerate(UNIT_ROWS))
N_SEM = 24 * len(CHUNKS) + 6 * len(UNITS)
SCALE = LOG2E * FEAT**-0.5
NT = (((1,), (1,)), ((), ()))


def nxt(a, by):
    return lax.rem(a + by, 4)


def by_lanes(op, a):
    return op(op(a[:, :128], a[:, 128:256]), op(a[:, 256:384], a[:, 384:]))


def attention_kernel(
    q_ref, k_ref, v_ref, gs_ref, w_ref, o_ref,
    qv, kb, vb, xa, wv, acc, ov, sizes, first, ssem, rsem, lsem,
):
    sp = lax.axis_index("sp")
    x = lax.axis_index("kv")
    c = lax.rem(sp, 2)
    y = lax.rem(sp // 2, 4)
    z = sp // 8

    def dev(z_, y_, c_, x_):
        return ((z_ * 4 + y_) * 2 + c_, x_)

    along_y = [dev(z, nxt(y, d), c, x) for d in (1, 3, 2)]
    along_z = [dev(nxt(z, d), y, c, x) for d in (1, 3, 2)]
    along_x = [dev(z, y, c, nxt(x, d)) for d in (1, 3, 2)]
    sibling = dev(z, y, 1 - c, x)

    peers = along_y + along_z + along_x + [sibling]
    barrier = pltpu.get_barrier_semaphore()
    for d in peers:
        pl.semaphore_signal(barrier, inc=1, device_id=d, device_id_type=MESH)
    size_copy = pltpu.make_async_copy(gs_ref, sizes, lsem.at[0])
    size_copy.start()
    q_copy = pltpu.make_async_copy(q_ref, qv, lsem.at[1])
    q_copy.start()
    w_copies = [
        pltpu.make_async_copy(
            w_ref.at[pl.ds(nxt(x, d) * COLS, COLS)], wv.at[i], lsem.at[2 + i]
        )
        for i, d in enumerate((0, 3, 1, 2))
    ]
    for w in w_copies:
        w.start()
    pl.semaphore_wait(barrier, len(peers))

    ids = {}
    pending = []

    def remote(key, src, dst, d):
        i = ids.setdefault(key, len(ids))
        return pltpu.make_async_remote_copy(
            src_ref=src, dst_ref=dst, send_sem=ssem.at[i], recv_sem=rsem.at[i],
            device_id=d, device_id_type=MESH,
        )

    def send(key, src, dst, d):
        r = remote(key, src, dst, d)
        r.start()
        pending.append(r)

    def recv(key, dst):
        remote(key, dst, dst, sibling).wait_recv()

    src = {"k": k_ref, "v": v_ref}

    def shard(t, f, r0, n):
        if t == "k":
            return kb.at[z, f, c, pl.ds(r0, n)]
        return vb.at[f, y, c, pl.ds(r0, n)]

    def line(t, s, core, r0, n):
        if t == "k":
            return kb.at[s, :, core, pl.ds(r0, n)]
        return vb.at[:, s, core, pl.ds(r0, n)]

    def firsts(t):
        return (y, along_y) if t == "k" else (z, along_z)

    def seconds(t):
        return (z, along_z) if t == "k" else (y, along_y)

    def own_copy(t, ci):
        r0, n = CHUNKS[ci]
        f, _ = firsts(t)
        return pltpu.make_async_copy(
            src[t].at[pl.ds(r0, n)], shard(t, f, r0, n), lsem.at[8 + 2 * ci + (t == "v")]
        )

    def kv_first(ci):
        r0, n = CHUNKS[ci]
        for t in "kv":
            f, to = firsts(t)
            for i in (2, 0, 1):
                send((t, ci, "f", i), src[t].at[pl.ds(r0, n)], shard(t, f, r0, n), to[i])
            own_copy(t, ci).start()

    def kv_second(ci):
        r0, n = CHUNKS[ci]
        for t in "kv":
            f, _ = firsts(t)
            s, to = seconds(t)
            for i, d in enumerate((3, 1, 2)):
                recv((t, ci, "f", i), shard(t, nxt(f, d), r0, n))
            own_copy(t, ci).wait()
            mine = line(t, s, c, r0, n)
            for i in (0, 1) if KV_RELAY[ci] else (2, 0, 1):
                send((t, ci, "s", i), mine, mine, to[i])
            send((t, ci, "c", 3), mine, mine, sibling)

    def kv_share_one(t, ci, i):
        r0, n = CHUNKS[ci]
        s, _ = seconds(t)
        got = line(t, nxt(s, (3, 1, 2)[i]), c, r0, n)
        send((t, ci, "c", i), got, got, sibling)

    def half_line(t, s, half, r0, n):
        if t == "k":
            return kb.at[s, pl.ds(2 * half, 2), c, pl.ds(r0, n)]
        return vb.at[pl.ds(2 * half, 2), s, c, pl.ds(r0, n)]

    def kv_relay(ci):
        r0, n = CHUNKS[ci]
        for i, d in enumerate((3, 1)):
            for t in "kv":
                s, to = seconds(t)
                recv((t, ci, "s", i), line(t, nxt(s, d), c, r0, n))
                if KV_RELAY[ci]:
                    part = half_line(t, nxt(s, d), i, r0, n)
                    send((t, ci, "g", i), part, part, to[i])
        for i in range(2):
            for t in "kv":
                kv_share_one(t, ci, i)

    def kv_share(ci):
        r0, n = CHUNKS[ci]
        for t in "kv":
            s, _ = seconds(t)
            far = nxt(s, 2)
            if KV_RELAY[ci]:
                for i in range(2):
                    recv((t, ci, "g", i), half_line(t, far, i, r0, n))
            else:
                recv((t, ci, "s", 2), line(t, far, c, r0, n))
            kv_share_one(t, ci, 2)

    def kv_ready(ci):
        r0, n = CHUNKS[ci]
        for i, d in enumerate((3, 1, 2, 0)):
            for t in "kv":
                s, _ = seconds(t)
                recv((t, ci, "c", i), line(t, nxt(s, d), 1 - c, r0, n))

    def halves(ci):
        r0, n = UNITS[ci]
        return pl.ds(r0, n // 2), pl.ds(r0 + n // 2, n // 2)

    def x_send(ci):
        a, b = halves(ci)
        right, left, _ = along_x
        send(("x", ci, "ra"), xa.at[0, a], xa.at[1, a], right)
        send(("x", ci, "lb"), xa.at[0, b], xa.at[2, b], left)
        send(("x", ci, "rb"), xa.at[0, b], xa.at[1, b], right)
        send(("x", ci, "la"), xa.at[0, a], xa.at[2, a], left)
        if not X_RELAY[ci]:
            both = pl.ds(*UNITS[ci])
            send(("x", ci, "far"), xa.at[0, both], xa.at[3, both], along_x[2])

    def x_forward(ci):
        a, b = halves(ci)
        right, left, _ = along_x
        recv(("x", ci, "ra"), xa.at[1, a])
        if X_RELAY[ci]:
            send(("x", ci, "fa"), xa.at[1, a], xa.at[3, a], right)
        recv(("x", ci, "lb"), xa.at[2, b])
        if X_RELAY[ci]:
            send(("x", ci, "fb"), xa.at[2, b], xa.at[3, b], left)

    def x_near(ci):
        a, b = halves(ci)
        recv(("x", ci, "rb"), xa.at[1, b])
        recv(("x", ci, "la"), xa.at[2, a])

    def x_far(ci):
        a, b = halves(ci)
        if X_RELAY[ci]:
            recv(("x", ci, "fa"), xa.at[3, a])
            recv(("x", ci, "fb"), xa.at[3, b])
        else:
            recv(("x", ci, "far"), xa.at[3, pl.ds(*UNITS[ci])])

    def make_table():
        q_copy.wait()
        size_copy.wait()
        listed = [sizes[i] for i in range(16)]

        @pl.loop(0, 32)
        def _(b):
            begin, total = 0, 0
            for size in listed:
                begin = jnp.where(total <= b, total, begin)
                total = total + size
            first[b] = begin

    def pair_rows(p):
        return pl.ds(p * PAIR, PAIR)

    def gathered(ref, p):
        return ref[:, :, :, pair_rows(p), :].reshape(KEYS, FEAT)

    def pair_bias(p, kp):
        lane = lax.broadcasted_iota(jnp.int32, (8, KEYS), 1)
        sub = lax.broadcasted_iota(jnp.int32, (8, KEYS), 0)
        key_id = kp * KEYS + ((lane // 8) % 2) * 256 + (lane // 16) * 8 + lane % 8
        biases = []
        for half in range(2):
            seen = key_id >= first[2 * p + half] * 256
            if kp == p:
                seen = seen & (key_id <= p * KEYS + half * 256 + sp * 8 + sub)
            biases.append(jnp.where(seen, 0.0, -1e30))
        return jnp.stack(biases)

    def scored(q, p_list, kp):
        s = lax.dot_general(q, gathered(kb, kp), NT, preferred_element_type=jnp.float32)
        bias = jnp.stack([pair_bias(p, kp)[None] for p in p_list])
        return (s.reshape(len(p_list), HEADS, 2, 8, KEYS) + bias).reshape(s.shape)

    def attend(t):
        m = HEADS * PAIR
        p0, p1 = 2 * t, 2 * t + 1
        q = jnp.concatenate(
            [qv[pair_rows(p), h * FEAT : (h + 1) * FEAT] for p in (p0, p1) for h in range(HEADS)], axis=0
        )
        middle = range(max(0, p0 - 3), p0 + 1)
        both = [scored(q, (p0, p1), kp) for kp in middle]
        edge1 = scored(q[m:], (p1,), p1)
        top1 = by_lanes(jnp.maximum, edge1)
        edge0 = None
        if p0 >= 4:
            edge0 = scored(q[:m], (p0,), p0 - 4)
            tops = jnp.concatenate([by_lanes(jnp.maximum, edge0), top1], axis=0)
        else:
            tops = jnp.concatenate([jnp.full((m, 128), -1e30, jnp.float32), top1], axis=0)
        for s in both:
            tops = jnp.maximum(tops, by_lanes(jnp.maximum, s))
        top = jnp.max(tops, axis=1, keepdims=True) * SCALE
        powers = jnp.exp2(edge1 * SCALE - top[m:])
        total1 = by_lanes(jnp.add, powers)
        out1 = jnp.dot(powers.astype(jnp.bfloat16), gathered(vb, p1), preferred_element_type=jnp.float32)
        if edge0 is not None:
            powers = jnp.exp2(edge0 * SCALE - top[:m])
            total0 = by_lanes(jnp.add, powers)
            out0 = jnp.dot(
                powers.astype(jnp.bfloat16), gathered(vb, p0 - 4), preferred_element_type=jnp.float32
            )
        else:
            total0 = jnp.zeros((m, 128), jnp.float32)
            out0 = jnp.zeros((m, FEAT), jnp.float32)
        total = jnp.concatenate([total0, total1], axis=0)
        out = jnp.concatenate([out0, out1], axis=0)
        for s, kp in zip(both, middle):
            powers = jnp.exp2(s * SCALE - top)
            total = total + by_lanes(jnp.add, powers)
            out = out + jnp.dot(
                powers.astype(jnp.bfloat16), gathered(vb, kp), preferred_element_type=jnp.float32
            )
        out = (out / jnp.sum(total, axis=1, keepdims=True)).astype(jnp.bfloat16)
        for i, p in enumerate((p0, p1)):
            for h in range(HEADS):
                at = i * m + h * PAIR
                xa[0, pair_rows(p), h * FEAT : (h + 1) * FEAT] = out[at : at + PAIR]

    def project(slot, r0, n, start=False):
        part = jnp.dot(xa[slot, r0 : r0 + n], wv[slot], preferred_element_type=jnp.float32)
        if start:
            acc[r0 : r0 + n] = part
        else:
            acc[r0 : r0 + n] += part

    out_copies = []

    def put_out(r0, n):
        ov[r0 : r0 + n] = acc[r0 : r0 + n].astype(jnp.bfloat16)
        copy = pltpu.make_async_copy(
            ov.at[pl.ds(r0, n)], o_ref.at[pl.ds(r0, n)], lsem.at[8 + 2 * len(CHUNKS) + len(out_copies)]
        )
        copy.start()
        out_copies.append(copy)

    last = len(UNITS) - TAIL
    r0 = UNITS[last][0]
    n = ROWS - r0

    def own_part():
        for w in w_copies:
            w.wait()
        project(0, 0, 256, start=True)

    def near_part():
        for i in range(last):
            x_near(i)
        project(1, 0, r0)
        project(2, 0, r0)

    def far_part():
        for i in range(last):
            x_far(i)
        project(3, 0, r0)
        put_out(0, r0)

    def near_last():
        for i in range(last, len(UNITS)):
            x_near(i)
        project(1, r0, n)
        project(2, r0, n)

    def far_last():
        for i in range(last, len(UNITS)):
            x_far(i)
        project(3, r0, n)
        put_out(r0, n)

    kv_first(0)
    kv_first(1)
    kv_first(2)
    kv_first(3)
    make_table()
    kv_second(0)
    kv_second(1)
    kv_second(2)
    kv_second(3)
    kv_relay(0)
    kv_share(0)
    kv_ready(0)
    attend(0)
    attend(1)
    x_send(0)
    kv_relay(1)
    kv_share(1)
    kv_relay(2)
    kv_ready(1)
    attend(2)
    kv_relay(3)
    attend(3)
    x_send(1)
    kv_share(2)
    x_forward(0)
    kv_ready(2)
    attend(4)
    attend(5)
    x_send(2)
    kv_share(3)
    x_forward(1)
    kv_ready(3)
    attend(6)
    attend(7)
    x_send(3)
    x_forward(2)
    own_part()
    x_forward(3)
    near_part()
    far_part()
    near_last()
    far_last()
    for copy in out_copies:
        copy.wait()
    for r in pending:
        r.wait_send()


def on_device(query_states, key_states, loader_value_rows, group_sizes, out_weight):
    anywhere = pl.BlockSpec(memory_space=pl.ANY)
    gathered = pltpu.VMEM((4, 4, 2, ROWS, FEAT), jnp.bfloat16)
    return pl.pallas_call(
        attention_kernel,
        out_shape=jax.ShapeDtypeStruct((ROWS, COLS), jnp.bfloat16),
        in_specs=[anywhere] * 5,
        out_specs=anywhere,
        scratch_shapes=[
            pltpu.VMEM((ROWS, COLS), jnp.bfloat16),
            gathered,
            gathered,
            pltpu.VMEM((4, ROWS, COLS), jnp.bfloat16),
            pltpu.VMEM((4, COLS, COLS), jnp.bfloat16),
            pltpu.VMEM((ROWS, COLS), jnp.float32),
            pltpu.VMEM((ROWS, COLS), jnp.bfloat16),
            pltpu.SMEM((16,), jnp.int32),
            pltpu.SMEM((32,), jnp.int32),
            pltpu.SemaphoreType.DMA((N_SEM,)),
            pltpu.SemaphoreType.DMA((N_SEM,)),
            pltpu.SemaphoreType.DMA((16 + 2 * len(CHUNKS),)),
        ],
        compiler_params=pltpu.CompilerParams(
            collective_id=0, has_side_effects=True, vmem_limit_bytes=56 << 20
        ),
    )(query_states, key_states, loader_value_rows, group_sizes, out_weight)


def solution(mesh):
    return jax.shard_map(
        on_device,
        mesh=mesh,
        in_specs=(P("sp", "kv"), P("sp", "kv"), P("sp", "kv"), P(), P(None, "kv")),
        out_specs=P("sp", "kv"),
        check_vma=False,
    )
```

```python
import functools

import jax
import jax.numpy as jnp
from jax import lax
from jax.experimental import pallas as pl
from jax.experimental.pallas import tpu as pltpu
from jax.sharding import PartitionSpec as P

MESH = pl.DeviceIdType.MESH
ROWS, FEAT, COLS, HEADS = 256, 128, 896, 7
PAIR = 16
KEYS = 512
LOG2E = 1.4426950408889634
QUAD = 32
CHUNK_ROWS = (64, 64, 64, 64)
CHUNKS = tuple((sum(CHUNK_ROWS[:i]), n) for i, n in enumerate(CHUNK_ROWS))
KV_RELAY = (0, 0, 1, 1)
X_RELAY = (1, 1, 1, 1)
TAIL = 1
UNIT_ROWS = (64, 64, 64, 64)
UNITS = tuple((sum(UNIT_ROWS[:i]), n) for i, n in enumerate(UNIT_ROWS))
N_SEM = 24 * len(CHUNKS) + 6 * len(UNITS)
SCALE = LOG2E * FEAT**-0.5
NT = (((1,), (1,)), ((), ()))


def nxt(a, by):
    return lax.rem(a + by, 4)


def by_lanes(op, a):
    return op(op(a[:, :128], a[:, 128:256]), op(a[:, 256:384], a[:, 384:]))


def attention_kernel(
    q_ref, k_ref, v_ref, gs_ref, w_ref, o_ref,
    qv, kb, vb, xa, wv, acc, ov, sizes, first, ssem, rsem, lsem,
):
    sp = lax.axis_index("sp")
    x = lax.axis_index("kv")
    c = lax.rem(sp, 2)
    y = lax.rem(sp // 2, 4)
    z = sp // 8

    def dev(z_, y_, c_, x_):
        return ((z_ * 4 + y_) * 2 + c_, x_)

    along_y = [dev(z, nxt(y, d), c, x) for d in (1, 3, 2)]
    along_z = [dev(nxt(z, d), y, c, x) for d in (1, 3, 2)]
    along_x = [dev(z, y, c, nxt(x, d)) for d in (1, 3, 2)]
    sibling = dev(z, y, 1 - c, x)

    peers = along_y + along_z + along_x + [sibling]
    barrier = pltpu.get_barrier_semaphore()
    for d in peers:
        pl.semaphore_signal(barrier, inc=1, device_id=d, device_id_type=MESH)
    size_copy = pltpu.make_async_copy(gs_ref, sizes, lsem.at[0])
    size_copy.start()
    q_copy = pltpu.make_async_copy(q_ref, qv, lsem.at[1])
    q_copy.start()
    w_copies = [
        pltpu.make_async_copy(
            w_ref.at[pl.ds(nxt(x, d) * COLS, COLS)], wv.at[i], lsem.at[2 + i]
        )
        for i, d in enumerate((0, 3, 1, 2))
    ]
    for w in w_copies:
        w.start()
    pl.semaphore_wait(barrier, len(peers))

    ids = {}
    pending = []

    def remote(key, src, dst, d):
        i = ids.setdefault(key, len(ids))
        return pltpu.make_async_remote_copy(
            src_ref=src, dst_ref=dst, send_sem=ssem.at[i], recv_sem=rsem.at[i],
            device_id=d, device_id_type=MESH,
        )

    def send(key, src, dst, d):
        r = remote(key, src, dst, d)
        r.start()
        pending.append(r)

    def recv(key, dst):
        remote(key, dst, dst, sibling).wait_recv()

    src = {"k": k_ref, "v": v_ref}

    def shard(t, f, r0, n):
        if t == "k":
            return kb.at[z, f, c, pl.ds(r0, n)]
        return vb.at[f, y, c, pl.ds(r0, n)]

    def line(t, s, core, r0, n):
        if t == "k":
            return kb.at[s, :, core, pl.ds(r0, n)]
        return vb.at[:, s, core, pl.ds(r0, n)]

    def firsts(t):
        return (y, along_y) if t == "k" else (z, along_z)

    def seconds(t):
        return (z, along_z) if t == "k" else (y, along_y)

    def own_copy(t, ci):
        r0, n = CHUNKS[ci]
        f, _ = firsts(t)
        return pltpu.make_async_copy(
            src[t].at[pl.ds(r0, n)], shard(t, f, r0, n), lsem.at[8 + 2 * ci + (t == "v")]
        )

    def kv_first(ci):
        r0, n = CHUNKS[ci]
        for t in "kv":
            f, to = firsts(t)
            for i in (2, 0, 1):
                send((t, ci, "f", i), src[t].at[pl.ds(r0, n)], shard(t, f, r0, n), to[i])
            own_copy(t, ci).start()

    def kv_second(ci):
        r0, n = CHUNKS[ci]
        for t in "kv":
            f, _ = firsts(t)
            s, to = seconds(t)
            for i, d in enumerate((3, 1, 2)):
                recv((t, ci, "f", i), shard(t, nxt(f, d), r0, n))
            own_copy(t, ci).wait()
            mine = line(t, s, c, r0, n)
            for i in (0, 1) if KV_RELAY[ci] else (2, 0, 1):
                send((t, ci, "s", i), mine, mine, to[i])
            send((t, ci, "c", 3), mine, mine, sibling)

    def kv_share_one(t, ci, i):
        r0, n = CHUNKS[ci]
        s, _ = seconds(t)
        got = line(t, nxt(s, (3, 1, 2)[i]), c, r0, n)
        send((t, ci, "c", i), got, got, sibling)

    def half_line(t, s, half, r0, n):
        if t == "k":
            return kb.at[s, pl.ds(2 * half, 2), c, pl.ds(r0, n)]
        return vb.at[pl.ds(2 * half, 2), s, c, pl.ds(r0, n)]

    def kv_relay(ci):
        r0, n = CHUNKS[ci]
        for i, d in enumerate((3, 1)):
            for t in "kv":
                s, to = seconds(t)
                recv((t, ci, "s", i), line(t, nxt(s, d), c, r0, n))
                if KV_RELAY[ci]:
                    part = half_line(t, nxt(s, d), i, r0, n)
                    send((t, ci, "g", i), part, part, to[i])
        for i in range(2):
            for t in "kv":
                kv_share_one(t, ci, i)

    def kv_share(ci):
        r0, n = CHUNKS[ci]
        for t in "kv":
            s, _ = seconds(t)
            far = nxt(s, 2)
            if KV_RELAY[ci]:
                for i in range(2):
                    recv((t, ci, "g", i), half_line(t, far, i, r0, n))
            else:
                recv((t, ci, "s", 2), line(t, far, c, r0, n))
            kv_share_one(t, ci, 2)

    def kv_ready(ci):
        r0, n = CHUNKS[ci]
        for i, d in enumerate((3, 1, 2, 0)):
            for t in "kv":
                s, _ = seconds(t)
                recv((t, ci, "c", i), line(t, nxt(s, d), 1 - c, r0, n))

    def halves(ci):
        r0, n = UNITS[ci]
        return pl.ds(r0, n // 2), pl.ds(r0 + n // 2, n // 2)

    def x_send(ci):
        a, b = halves(ci)
        right, left, _ = along_x
        send(("x", ci, "ra"), xa.at[0, a], xa.at[1, a], right)
        send(("x", ci, "lb"), xa.at[0, b], xa.at[2, b], left)
        send(("x", ci, "rb"), xa.at[0, b], xa.at[1, b], right)
        send(("x", ci, "la"), xa.at[0, a], xa.at[2, a], left)
        if not X_RELAY[ci]:
            both = pl.ds(*UNITS[ci])
            send(("x", ci, "far"), xa.at[0, both], xa.at[3, both], along_x[2])

    def x_forward(ci):
        a, b = halves(ci)
        right, left, _ = along_x
        recv(("x", ci, "ra"), xa.at[1, a])
        if X_RELAY[ci]:
            send(("x", ci, "fa"), xa.at[1, a], xa.at[3, a], right)
        recv(("x", ci, "lb"), xa.at[2, b])
        if X_RELAY[ci]:
            send(("x", ci, "fb"), xa.at[2, b], xa.at[3, b], left)

    def x_near(ci):
        a, b = halves(ci)
        recv(("x", ci, "rb"), xa.at[1, b])
        recv(("x", ci, "la"), xa.at[2, a])

    def x_far(ci):
        a, b = halves(ci)
        if X_RELAY[ci]:
            recv(("x", ci, "fa"), xa.at[3, a])
            recv(("x", ci, "fb"), xa.at[3, b])
        else:
            recv(("x", ci, "far"), xa.at[3, pl.ds(*UNITS[ci])])

    def make_table():
        q_copy.wait()
        size_copy.wait()
        listed = [sizes[i] for i in range(16)]

        @pl.loop(0, 32)
        def _(b):
            begin, total = 0, 0
            for size in listed:
                begin = jnp.where(total <= b, total, begin)
                total = total + size
            first[b] = begin

    def pair_rows(p):
        return pl.ds(p * PAIR, PAIR)

    def gathered(ref, p):
        return ref[:, :, :, pair_rows(p), :].reshape(KEYS, FEAT)

    def pair_bias(p, kp):
        lane = lax.broadcasted_iota(jnp.int32, (8, KEYS), 1)
        sub = lax.broadcasted_iota(jnp.int32, (8, KEYS), 0)
        key_id = kp * KEYS + ((lane // 8) % 2) * 256 + (lane // 16) * 8 + lane % 8
        biases = []
        for half in range(2):
            seen = key_id >= first[2 * p + half] * 256
            if kp == p:
                seen = seen & (key_id <= p * KEYS + half * 256 + sp * 8 + sub)
            biases.append(jnp.where(seen, 0.0, -1e30))
        return jnp.stack(biases)

    def scored(q, p_list, kp):
        s = lax.dot_general(q, gathered(kb, kp), NT, preferred_element_type=jnp.float32)
        bias = jnp.stack([pair_bias(p, kp)[None] for p in p_list])
        return (s.reshape(len(p_list), HEADS, 2, 8, KEYS) + bias).reshape(s.shape)

    def attend(t):
        m = HEADS * PAIR
        p0, p1 = 2 * t, 2 * t + 1
        q = jnp.concatenate(
            [qv[pair_rows(p), h * FEAT : (h + 1) * FEAT] for p in (p0, p1) for h in range(HEADS)], axis=0
        )
        middle = range(max(0, p0 - 3), p0 + 1)
        both = [scored(q, (p0, p1), kp) for kp in middle]
        edge1 = scored(q[m:], (p1,), p1)
        top1 = by_lanes(jnp.maximum, edge1)
        edge0 = None
        if p0 >= 4:
            edge0 = scored(q[:m], (p0,), p0 - 4)
            tops = jnp.concatenate([by_lanes(jnp.maximum, edge0), top1], axis=0)
        else:
            tops = jnp.concatenate([jnp.full((m, 128), -1e30, jnp.float32), top1], axis=0)
        for s in both:
            tops = jnp.maximum(tops, by_lanes(jnp.maximum, s))
        top = jnp.max(tops, axis=1, keepdims=True) * SCALE
        powers = jnp.exp2(edge1 * SCALE - top[m:])
        total1 = by_lanes(jnp.add, powers)
        out1 = jnp.dot(powers.astype(jnp.bfloat16), gathered(vb, p1), preferred_element_type=jnp.float32)
        if edge0 is not None:
            powers = jnp.exp2(edge0 * SCALE - top[:m])
            total0 = by_lanes(jnp.add, powers)
            out0 = jnp.dot(
                powers.astype(jnp.bfloat16), gathered(vb, p0 - 4), preferred_element_type=jnp.float32
            )
        else:
            total0 = jnp.zeros((m, 128), jnp.float32)
            out0 = jnp.zeros((m, FEAT), jnp.float32)
        total = jnp.concatenate([total0, total1], axis=0)
        out = jnp.concatenate([out0, out1], axis=0)
        for s, kp in zip(both, middle):
            powers = jnp.exp2(s * SCALE - top)
            total = total + by_lanes(jnp.add, powers)
            out = out + jnp.dot(
                powers.astype(jnp.bfloat16), gathered(vb, kp), preferred_element_type=jnp.float32
            )
        out = (out / jnp.sum(total, axis=1, keepdims=True)).astype(jnp.bfloat16)
        for i, p in enumerate((p0, p1)):
            for h in range(HEADS):
                at = i * m + h * PAIR
                xa[0, pair_rows(p), h * FEAT : (h + 1) * FEAT] = out[at : at + PAIR]

    def project(slot, r0, n, start=False):
        part = jnp.dot(xa[slot, r0 : r0 + n], wv[slot], preferred_element_type=jnp.float32)
        if start:
            acc[r0 : r0 + n] = part
        else:
            acc[r0 : r0 + n] += part

    out_copies = []

    def put_out(r0, n):
        ov[r0 : r0 + n] = acc[r0 : r0 + n].astype(jnp.bfloat16)
        copy = pltpu.make_async_copy(
            ov.at[pl.ds(r0, n)], o_ref.at[pl.ds(r0, n)], lsem.at[8 + 2 * len(CHUNKS) + len(out_copies)]
        )
        copy.start()
        out_copies.append(copy)

    last = len(UNITS) - TAIL
    r0 = UNITS[last][0]
    n = ROWS - r0

    def own_part():
        for w in w_copies:
            w.wait()
        project(0, 0, 256, start=True)

    def near_part():
        for i in range(last):
            x_near(i)
        project(1, 0, r0)
        project(2, 0, r0)

    def far_part():
        for i in range(last):
            x_far(i)
        project(3, 0, r0)
        put_out(0, r0)

    def near_last():
        for i in range(last, len(UNITS)):
            x_near(i)
        project(1, r0, n)
        project(2, r0, n)

    def far_last():
        for i in range(last, len(UNITS)):
            x_far(i)
        project(3, r0, n)
        put_out(r0, n)

    kv_first(0)
    kv_first(1)
    kv_first(2)
    kv_first(3)
    make_table()
    kv_second(0)
    kv_second(1)
    kv_second(2)
    kv_second(3)
    kv_relay(0)
    kv_share(0)
    kv_ready(0)
    attend(0)
    attend(1)
    x_send(0)
    kv_relay(1)
    kv_share(1)
    kv_relay(2)
    kv_ready(1)
    kv_relay(3)
    attend(2)
    attend(3)
    x_send(1)
    kv_share(2)
    x_forward(0)
    kv_ready(2)
    attend(4)
    attend(5)
    x_send(2)
    kv_share(3)
    x_forward(1)
    kv_ready(3)
    attend(6)
    attend(7)
    x_send(3)
    x_forward(2)
    own_part()
    x_forward(3)
    near_part()
    far_part()
    near_last()
    far_last()
    for copy in out_copies:
        copy.wait()
    for r in pending:
        r.wait_send()


def on_device(query_states, key_states, loader_value_rows, group_sizes, out_weight):
    anywhere = pl.BlockSpec(memory_space=pl.ANY)
    gathered = pltpu.VMEM((4, 4, 2, ROWS, FEAT), jnp.bfloat16)
    return pl.pallas_call(
        attention_kernel,
        out_shape=jax.ShapeDtypeStruct((ROWS, COLS), jnp.bfloat16),
        in_specs=[anywhere] * 5,
        out_specs=anywhere,
        scratch_shapes=[
            pltpu.VMEM((ROWS, COLS), jnp.bfloat16),
            gathered,
            gathered,
            pltpu.VMEM((4, ROWS, COLS), jnp.bfloat16),
            pltpu.VMEM((4, COLS, COLS), jnp.bfloat16),
            pltpu.VMEM((ROWS, COLS), jnp.float32),
            pltpu.VMEM((ROWS, COLS), jnp.bfloat16),
            pltpu.SMEM((16,), jnp.int32),
            pltpu.SMEM((32,), jnp.int32),
            pltpu.SemaphoreType.DMA((N_SEM,)),
            pltpu.SemaphoreType.DMA((N_SEM,)),
            pltpu.SemaphoreType.DMA((16 + 2 * len(CHUNKS),)),
        ],
        compiler_params=pltpu.CompilerParams(
            collective_id=0, has_side_effects=True, vmem_limit_bytes=56 << 20
        ),
    )(query_states, key_states, loader_value_rows, group_sizes, out_weight)


def solution(mesh):
    return jax.shard_map(
        on_device,
        mesh=mesh,
        in_specs=(P("sp", "kv"), P("sp", "kv"), P("sp", "kv"), P(), P(None, "kv")),
        out_specs=P("sp", "kv"),
        check_vma=False,
    )
```
